1024 devices in a mesh: row: 64 (over x, z_lo, core), col: 16 (over y, z_hi).
Axes of the slice: x: 4, y: 4, z: 32 (z_hi: 4, z_lo: 8; z = z_hi * 8 + z_lo), core: 2. Of those that a mesh axis runs over, the one named last changes fastest.
Arguments:
- hamilton: bfloat16 [4096, 4096], P('row', 'col'), may hold values from -17 to 17, as said below
- block_flags: int32 [64, 64], P('row', 'col'), may hold values from 0 to 1, as said below
Outputs:
- next_iterate: float32 [4096, 4096], P('row', 'col')
The draws below stay inside these ranges and needn't reach their ends.
Inputs may be any that keep to these rules, and one draw needn't show every extreme that they name: The hamilton matrix is real and symmetric. `block_flags`: block i sits at cell (p_i // 16, p_i % 16) of a periodic grid of 4 by 16 cells, where p is a permutation of the block indices; a block is kept only if both periodic cell distances between its row and column blocks are at most 2, and always if both are at most 1. The flags are symmetric.
All inputs are finite; a program needn't handle non-finite values.
Results may differ from the reference program's by a relative error of at most 0.0052.
Values may be sent and summed in bfloat16 or wider, within the bound.
A program may use at most 32 MiB of HBM per device.

```python
import jax
import jax.numpy as jnp

BS = 64
NB = 64
CELLS_Y = 16
ORDER = 4096


def draw_hamilton(key, part):
    key = jax.random.fold_in(key, 5)
    first_key = jax.random.fold_in(key, 0)
    base = jax.random.normal(first_key, (ORDER, ORDER), jnp.float32)
    values = jnp.clip((base + base.T) * 0.7071, -4.0, 4.0)
    return values.astype(jnp.bfloat16)


def draw_block_flags(key, part):
    key = jax.random.fold_in(key, 11)
    first_key, second_key, third_key = jax.random.split(key, 3)
    places = jax.random.permutation(third_key, NB).astype(jnp.int32)
    height = NB // CELLS_Y
    grid_a = places // CELLS_Y
    grid_b = places % CELLS_Y
    reach_a = 1 + jax.random.randint(first_key, (NB,), 0, 2, dtype=jnp.int32)
    reach_b = 1 + jax.random.randint(second_key, (NB,), 0, 2, dtype=jnp.int32)
    apart_a = jnp.abs(grid_a[:, None] - grid_a[None, :])
    apart_a = jnp.minimum(apart_a, height - apart_a)
    apart_b = jnp.abs(grid_b[:, None] - grid_b[None, :])
    apart_b = jnp.minimum(apart_b, CELLS_Y - apart_b)
    near_a = apart_a <= jnp.maximum(reach_a[:, None], reach_a[None, :])
    near_b = apart_b <= jnp.maximum(reach_b[:, None], reach_b[None, :])
    return (near_a & near_b).astype(jnp.int32)


def setup_inputs(seed: int = 0) -> dict:
    key_list = jax.random.split(jax.random.key(seed), 3)
    hamilton = draw_hamilton(jax.random.fold_in(key_list[2], 71), 0)
    block_flags = draw_block_flags(jax.random.fold_in(key_list[2], 71), 0)
    return {"hamilton": hamilton, "block_flags": block_flags}


def widen(block_flags, size):
    return jnp.repeat(jnp.repeat(block_flags, size, 0), size, 1)

def reference(hamilton, block_flags):
    keeper = widen(block_flags, BS) > 0
    masked = jnp.where(keeper, hamilton, jnp.zeros_like(hamilton))
    wide = masked.astype(jnp.float32)
    squares = jnp.sum(wide * wide)
    factor = jnp.sqrt(jnp.float32(ORDER) / squares)
    xmat = (wide * factor).astype(jnp.bfloat16)
    first = jnp.dot(xmat, xmat, preferred_element_type=jnp.float32).astype(jnp.bfloat16)
    second = jnp.dot(first, xmat, preferred_element_type=jnp.float32)
    return 16.0 * (1.5 * xmat.astype(jnp.float32) - 0.5 * second)
```

```python
import jax
import jax.numpy as jnp
from jax import lax
from jax.experimental import pallas as pl
from jax.experimental.pallas import tpu as pltpu
from jax.sharding import PartitionSpec as P

MESH = pl.DeviceIdType.MESH
NX, NY, NZL, NZH, NC = 4, 4, 8, 4, 2
BS = 64
WIDE = 256
ORDER = 4096


def kernel(flag_ref, h_ref, out_ref, panel, rowp, firstp, xpanel, p1, p2, p3, send, recv):
    row = lax.axis_index("row")
    col = lax.axis_index("col")
    x = lax.div(row, NZL * NC)
    zl = lax.rem(lax.div(row, NC), NZL)
    c = lax.rem(row, NC)
    y = lax.div(col, NZH)
    zh = lax.rem(col, NZH)

    def dev(x=x, y=y, zl=zl, zh=zh, c=c):
        return ((x * NZL + zl) * NC + c, y * NZH + zh)

    def zl_peer(d):
        return dev(zl=lax.rem(zl + d, NZL))

    def zh_peer(d):
        return dev(zh=lax.rem(zh + d, NZH))

    def x_peer(d):
        return dev(x=lax.rem(x + d, NX))

    def y_peer(d):
        return dev(y=lax.rem(y + d, NY))

    def xc_peer(d):
        at = lax.rem(x * NC + c + d, NX * NC)
        return dev(x=lax.div(at, NC), c=lax.rem(at, NC))

    def col_peer(d):
        at = lax.rem(col + d, NY * NZH)
        return (row, at)

    other = dev(c=1 - c)

    barrier = pltpu.get_barrier_semaphore()

    def greet(count, peer):
        def step(d, carry):
            pl.semaphore_signal(barrier, inc=1, device_id=peer(d), device_id_type=MESH)
            return carry

        lax.fori_loop(1, count, step, 0)

    greet(NX * NC, xc_peer)
    greet(NZL, zl_peer)
    greet(NY * NZH, col_peer)

    def spread(count, peer, ref, k):
        def step(d, carry):
            pltpu.make_async_remote_copy(
                src_ref=ref,
                dst_ref=ref,
                send_sem=send.at[k],
                recv_sem=recv.at[k],
                device_id=peer(d),
                device_id_type=MESH,
            ).start()
            return carry

        lax.fori_loop(1, count, step, 0)

    def await_bytes(view, sem):
        pltpu.make_async_copy(view, view, sem).wait()

    total = jnp.zeros((1, 128), jnp.float32)
    for b in range(4):
        part = h_ref[:, b * BS:(b + 1) * BS]
        part = jnp.where(flag_ref[0, b] > 0, part, jnp.zeros_like(part))
        panel[x, zl, c, :, b * BS:(b + 1) * BS] = part
        rowp[y, zh, :, b * BS:(b + 1) * BS] = part
    wide = rowp[y, zh].astype(jnp.float32)
    wide = wide * wide
    half = wide[:, :128] + wide[:, 128:]
    total = jnp.sum(half, axis=0, keepdims=True)
    p1[x * NC + c] = total

    pl.semaphore_wait(barrier, (NX * NC - 1) + (NZL - 1) + (NY * NZH - 1))

    spread(NX * NC, xc_peer, p1.at[x * NC + c], 0)
    spread(NZH, zh_peer, rowp.at[y, zh], 1)
    spread(NZL, zl_peer, panel.at[x, zl, c], 2)

    await_bytes(p1.at[pl.ds(0, 7)], recv.at[0])
    p2[zl] = jnp.sum(p1[...], axis=0)
    spread(NZL, zl_peer, p2.at[zl], 3)
    await_bytes(p2.at[pl.ds(0, 7)], recv.at[3])
    p3[col] = jnp.sum(p2[...], axis=0)
    spread(NY * NZH, col_peer, p3.at[col], 4)

    await_bytes(rowp.at[0, pl.ds(0, 3)], recv.at[1])
    spread(NY, y_peer, rowp.at[y], 5)
    await_bytes(panel.at[0, pl.ds(0, 7), 0], recv.at[2])
    spread(NX, x_peer, panel.at[x, :, c], 6)

    def across(ref, k):
        copy = pltpu.make_async_remote_copy(
            src_ref=ref,
            dst_ref=ref,
            send_sem=send.at[k],
            recv_sem=recv.at[k],
            device_id=other,
            device_id_type=MESH,
        )
        copy.start()

    across(panel.at[x, :, c], 7)

    await_bytes(p3.at[pl.ds(0, 15)], recv.at[4])
    squares = jnp.sum(jnp.sum(p3[...], axis=0), axis=1, keepdims=True)
    factor = jnp.sqrt(jnp.float32(ORDER) / squares)

    await_bytes(panel.at[pl.ds(0, 3), :, 0], recv.at[6])
    for d in range(1, NX):
        at = lax.rem(x + d, NX)
        across(panel.at[at, :, c], 7 + d)
    await_bytes(rowp.at[pl.ds(0, 3)], recv.at[5])
    for d in range(NX):
        await_bytes(panel.at[0, :, 0], recv.at[7 + d])

    acc = jnp.zeros((BS, WIDE), jnp.float32)
    for j in range(16):
        left = (rowp[j // 4, j % 4].astype(jnp.float32) * factor).astype(jnp.bfloat16)
        chunk = panel[j // 4, (j % 4) * 2:(j % 4) * 2 + 2].reshape(WIDE, WIDE)
        right = (chunk.astype(jnp.float32) * factor).astype(jnp.bfloat16)
        xpanel[j] = right
        acc += jnp.dot(left, right, preferred_element_type=jnp.float32)
    firstp[y, zh] = acc.astype(jnp.bfloat16)

    spread(NZH, zh_peer, firstp.at[y, zh], 11)
    await_bytes(firstp.at[0, pl.ds(0, 3)], recv.at[11])
    spread(NY, y_peer, firstp.at[y], 12)
    await_bytes(firstp.at[pl.ds(0, 3)], recv.at[12])

    acc = jnp.zeros((BS, WIDE), jnp.float32)
    for j in range(16):
        acc += jnp.dot(firstp[j // 4, j % 4], xpanel[j], preferred_element_type=jnp.float32)
    own = (rowp[y, zh].astype(jnp.float32) * factor).astype(jnp.bfloat16).astype(jnp.float32)
    out_ref[...] = 16.0 * (1.5 * own - 0.5 * acc)

    await_bytes(p1.at[pl.ds(0, 7)], send.at[0])
    await_bytes(rowp.at[0, pl.ds(0, 3)], send.at[1])
    await_bytes(panel.at[0, pl.ds(0, 7), 0], send.at[2])
    await_bytes(p2.at[pl.ds(0, 7)], send.at[3])
    await_bytes(p3.at[pl.ds(0, 15)], send.at[4])
    await_bytes(rowp.at[pl.ds(0, 3)], send.at[5])
    await_bytes(panel.at[pl.ds(0, 3), :, 0], send.at[6])
    for d in range(NX):
        await_bytes(panel.at[0, :, 0], send.at[7 + d])
    await_bytes(firstp.at[0, pl.ds(0, 3)], send.at[11])
    await_bytes(firstp.at[pl.ds(0, 3)], send.at[12])


def body(hamilton, block_flags):
    return pl.pallas_call(
        kernel,
        out_shape=jax.ShapeDtypeStruct((BS, WIDE), jnp.float32),
        in_specs=[
            pl.BlockSpec(memory_space=pltpu.SMEM),
            pl.BlockSpec(memory_space=pltpu.VMEM),
        ],
        out_specs=pl.BlockSpec(memory_space=pltpu.VMEM),
        scratch_shapes=[
            pltpu.VMEM((NX, NZL, NC, BS, WIDE), jnp.bfloat16),
            pltpu.VMEM((NY, NZH, BS, WIDE), jnp.bfloat16),
            pltpu.VMEM((NY, NZH, BS, WIDE), jnp.bfloat16),
            pltpu.VMEM((16, WIDE, WIDE), jnp.bfloat16),
            pltpu.VMEM((8, 1, 128), jnp.float32),
            pltpu.VMEM((8, 1, 128), jnp.float32),
            pltpu.VMEM((16, 1, 128), jnp.float32),
            pltpu.SemaphoreType.DMA((13,)),
            pltpu.SemaphoreType.DMA((13,)),
        ],
        compiler_params=pltpu.CompilerParams(
            collective_id=0, has_side_effects=True, vmem_limit_bytes=32 * 1024 * 1024
        ),
    )(block_flags, hamilton)


def solution(mesh):
    in_specs = (P("row", "col"), P("row", "col"))
    out_specs = P("row", "col")
    return jax.shard_map(body, mesh=mesh, in_specs=in_specs, out_specs=out_specs, check_vma=False)
```

```python
import jax
import jax.numpy as jnp
from jax import lax
from jax.experimental import pallas as pl
from jax.experimental.pallas import tpu as pltpu
from jax.sharding import PartitionSpec as P

MESH = pl.DeviceIdType.MESH
NX, NY, NZL, NZH, NC = 4, 4, 8, 4, 2
NZ = NZL * NZH
BS = 64
WIDE = 256
ORDER = 4096

P1, P2, P3, P4 = 0, 1, 2, 3
ROW_L, ROW_R, ROW_LF, ROW_RF = 4, 5, 6, 7
ROW_Y0, ROW_Y1, ROW_Y2 = 8, 9, 10
COL_NEAR, COL_FAR, X_NEAR, X_FAR, C_NEAR, C_FAR = 11, 12, 13, 14, 15, 16
F_1, F_2, F_Y0, F_Y1, F_Y2 = 17, 18, 19, 20, 21
N_SEM = 22


def kernel(flag_ref, h_ref, out_ref, panel, rowp, firstp, xpanel, p1, p2, p3, p4, send, recv):
    row = lax.axis_index("row")
    col = lax.axis_index("col")
    x = lax.div(row, NZL * NC)
    zl = lax.rem(lax.div(row, NC), NZL)
    c = lax.rem(row, NC)
    y = lax.div(col, NZH)
    zh = lax.rem(col, NZH)
    z = zh * NZL + zl
    near = lax.div(zl, 4) * 4
    far = 4 - near
    left = lax.rem(zh + 3, NZH)
    right = lax.rem(zh + 1, NZH)
    across = lax.rem(zh + 2, NZH)

    def dev(x=x, y=y, zl=zl, zh=zh, c=c):
        return ((x * NZL + zl) * NC + c, y * NZH + zh)

    def z_peer(d):
        at = lax.rem(z + d + NZ, NZ)
        return dev(zl=lax.rem(at, NZL), zh=lax.div(at, NZL))

    def x_peer(d):
        return dev(x=lax.rem(x + d, NX))

    def y_peer(d):
        return dev(y=lax.rem(y + d, NY))

    def xc_peer(d):
        at = lax.rem(x * NC + c + d, NX * NC)
        return dev(x=lax.div(at, NC), c=lax.rem(at, NC))

    def put(ref, k, to, dst=None):
        pltpu.make_async_remote_copy(
            src_ref=ref,
            dst_ref=ref if dst is None else dst,
            send_sem=send.at[k],
            recv_sem=recv.at[k],
            device_id=to,
            device_id_type=MESH,
        ).start()

    def take(view, k):
        pltpu.make_async_copy(view, view, recv.at[k]).wait()

    def sent(view, k):
        pltpu.make_async_copy(view, view, send.at[k]).wait()

    barrier = pltpu.get_barrier_semaphore()

    def greet(first, last, peer):
        def step(d, carry):
            pl.semaphore_signal(barrier, inc=1, device_id=peer(d), device_id_type=MESH)
            return carry

        lax.fori_loop(first, last, step, 0)

    greet(1, 9, z_peer)
    greet(-8, 0, z_peer)
    greet(1, NX * NC, xc_peer)
    greet(1, NY, y_peer)

    for b in range(4):
        part = h_ref[:, b * BS:(b + 1) * BS]
        part = jnp.where(flag_ref[0, b] > 0, part, jnp.zeros_like(part))
        panel[x, zl, c, :, b * BS:(b + 1) * BS] = part
        rowp[y, zh, :, b * BS:(b + 1) * BS] = part
    wide = rowp[y, zh].astype(jnp.float32)
    wide = wide * wide
    p1[x * NC + c] = jnp.sum(wide[:, :128] + wide[:, 128:], axis=0, keepdims=True)

    pl.semaphore_wait(barrier, 16 + (NX * NC - 1) + (NY - 1))

    for d in range(1, NX * NC):
        put(p1.at[x * NC + c], P1, xc_peer(d))
    own_row = rowp.at[y, zh]
    put(own_row, ROW_L, dev(zh=right))
    put(own_row, ROW_R, dev(zh=left))
    own_col = panel.at[x, zl, c]
    for d in range(4):
        put(own_col, COL_FAR, dev(zl=far + lax.rem(zl + d, 4)))
    for d in range(1, 4):
        put(own_col, COL_NEAR, dev(zl=near + lax.rem(zl + d, 4)))
    for d in range(1, NY):
        put(own_row, ROW_Y0, y_peer(d))

    take(p1.at[pl.ds(0, 7)], P1)
    p2[y] = jnp.sum(p1[...], axis=0)
    for d in range(1, NY):
        put(p2.at[y], P2, y_peer(d))
    take(p2.at[pl.ds(0, 3)], P2)
    p3[7] = jnp.sum(p2[...], axis=0)
    for d in range(-8, 8):
        if d != 0:
            put(p3.at[7], P3, z_peer(d), p3.at[7 - d])

    take(panel.at[0, pl.ds(0, 3), 0], COL_NEAR)
    batch = panel.at[x, pl.ds(near, 4), c]
    for d in (2, 1, 3):
        put(batch, X_NEAR, x_peer(d))

    half = BS // 2
    take(own_row, ROW_L)
    put(rowp.at[y, left, pl.ds(0, half)], ROW_LF, dev(zh=right))
    take(own_row, ROW_R)
    put(rowp.at[y, right, pl.ds(half, half)], ROW_RF, dev(zh=left))
    for d in range(1, NY):
        put(rowp.at[y, left], ROW_Y1, y_peer(d))
        put(rowp.at[y, right], ROW_Y1, y_peer(d))

    take(panel.at[pl.ds(0, 3), pl.ds(0, 4), 0], X_NEAR)
    put(panel.at[:, pl.ds(near, 4), c], C_NEAR, dev(c=1 - c))
    take(panel.at[0, pl.ds(0, 4), 0], COL_FAR)
    batch = panel.at[x, pl.ds(far, 4), c]
    for d in (2, 1, 3):
        put(batch, X_FAR, x_peer(d))

    take(p3.at[pl.ds(0, 15)], P3)
    p4[2] = jnp.sum(p3[...], axis=0)
    put(p4.at[2], P4, dev(zh=right), p4.at[0])
    put(p4.at[2], P4, dev(zh=left), p4.at[1])

    take(rowp.at[0, 0, pl.ds(0, half)], ROW_LF)
    take(rowp.at[0, 0, pl.ds(0, half)], ROW_RF)
    for d in range(1, NY):
        put(rowp.at[y, across], ROW_Y2, y_peer(d))

    take(panel.at[pl.ds(0, 3), pl.ds(0, 4), 0], X_FAR)
    put(panel.at[:, pl.ds(far, 4), c], C_FAR, dev(c=1 - c))
    take(p4.at[pl.ds(0, 2)], P4)
    squares = jnp.sum(p4[0] + p4[1], axis=1, keepdims=True)
    factor = jnp.sqrt(jnp.float32(ORDER) / squares)
    take(panel.at[:, pl.ds(0, 4), 0], C_NEAR)
    take(panel.at[:, pl.ds(0, 4), 0], C_FAR)
    take(rowp.at[0, pl.ds(0, 3)], ROW_Y0)
    take(rowp.at[pl.ds(0, 3), pl.ds(0, 2)], ROW_Y1)
    take(rowp.at[0, pl.ds(0, 3)], ROW_Y2)

    acc = jnp.zeros((BS, WIDE), jnp.float32)
    for j in range(16):
        lhs = (rowp[j // 4, j % 4].astype(jnp.float32) * factor).astype(jnp.bfloat16)
        rhs = panel[j // 4, (j % 4) * 2:(j % 4) * 2 + 2].reshape(WIDE, WIDE)
        rhs = (rhs.astype(jnp.float32) * factor).astype(jnp.bfloat16)
        xpanel[j] = rhs
        acc += jnp.dot(lhs, rhs, preferred_element_type=jnp.float32)
    firstp[y, zh] = acc.astype(jnp.bfloat16)

    own_first = firstp.at[y, zh]
    put(own_first, F_2, dev(zh=across))
    put(own_first, F_1, dev(zh=right))
    put(own_first, F_1, dev(zh=left))
    for d in range(1, NY):
        put(own_first, F_Y0, y_peer(d))

    def dots(h):
        total = jnp.zeros((BS, WIDE), jnp.float32)
        for i in range(NY):
            total += jnp.dot(firstp[i, h], xpanel[i * NZH + h], preferred_element_type=jnp.float32)
        return total

    take(firstp.at[0, pl.ds(0, 3)], F_Y0)
    acc = dots(zh)
    take(firstp.at[0, pl.ds(0, 2)], F_1)
    for d in range(1, NY):
        put(firstp.at[y, left], F_Y1, y_peer(d))
        put(firstp.at[y, right], F_Y1, y_peer(d))
    take(firstp.at[pl.ds(0, 3), pl.ds(0, 2)], F_Y1)
    acc += dots(left) + dots(right)
    take(own_first, F_2)
    for d in range(1, NY):
        put(firstp.at[y, across], F_Y2, y_peer(d))
    own = (rowp[y, zh].astype(jnp.float32) * factor).astype(jnp.bfloat16).astype(jnp.float32)
    acc = 1.5 * own - 0.5 * acc
    take(firstp.at[0, pl.ds(0, 3)], F_Y2)
    out_ref[...] = 16.0 * (acc - 0.5 * dots(across))

    sent(p1.at[pl.ds(0, 7)], P1)
    sent(p2.at[pl.ds(0, 3)], P2)
    sent(p3.at[pl.ds(0, 15)], P3)
    sent(p4.at[pl.ds(0, 2)], P4)
    sent(own_row, ROW_L)
    sent(own_row, ROW_R)
    sent(rowp.at[0, 0, pl.ds(0, half)], ROW_LF)
    sent(rowp.at[0, 0, pl.ds(0, half)], ROW_RF)
    sent(rowp.at[0, pl.ds(0, 3)], ROW_Y0)
    sent(rowp.at[pl.ds(0, 3), pl.ds(0, 2)], ROW_Y1)
    sent(rowp.at[0, pl.ds(0, 3)], ROW_Y2)
    sent(panel.at[0, pl.ds(0, 3), 0], COL_NEAR)
    sent(panel.at[0, pl.ds(0, 4), 0], COL_FAR)
    sent(panel.at[pl.ds(0, 3), pl.ds(0, 4), 0], X_NEAR)
    sent(panel.at[pl.ds(0, 3), pl.ds(0, 4), 0], X_FAR)
    sent(panel.at[:, pl.ds(0, 4), 0], C_NEAR)
    sent(panel.at[:, pl.ds(0, 4), 0], C_FAR)
    sent(firstp.at[0, pl.ds(0, 2)], F_1)
    sent(own_first, F_2)
    sent(firstp.at[0, pl.ds(0, 3)], F_Y0)
    sent(firstp.at[pl.ds(0, 3), pl.ds(0, 2)], F_Y1)
    sent(firstp.at[0, pl.ds(0, 3)], F_Y2)


SCRATCH = [
    pltpu.VMEM((NX, NZL, NC, BS, WIDE), jnp.bfloat16),
    pltpu.VMEM((NY, NZH, BS, WIDE), jnp.bfloat16),
    pltpu.VMEM((NY, NZH, BS, WIDE), jnp.bfloat16),
    pltpu.VMEM((16, WIDE, WIDE), jnp.bfloat16),
    pltpu.VMEM((NX * NC, 1, 128), jnp.float32),
    pltpu.VMEM((NY, 1, 128), jnp.float32),
    pltpu.VMEM((16, 1, 128), jnp.float32),
    pltpu.VMEM((3, 1, 128), jnp.float32),
    pltpu.SemaphoreType.DMA((N_SEM,)),
    pltpu.SemaphoreType.DMA((N_SEM,)),
]


def body(hamilton, block_flags):
    return pl.pallas_call(
        kernel,
        out_shape=jax.ShapeDtypeStruct((BS, WIDE), jnp.float32),
        in_specs=[
            pl.BlockSpec(memory_space=pltpu.SMEM),
            pl.BlockSpec(memory_space=pltpu.VMEM),
        ],
        out_specs=pl.BlockSpec(memory_space=pltpu.VMEM),
        scratch_shapes=SCRATCH,
        compiler_params=pltpu.CompilerParams(
            collective_id=0, has_side_effects=True, vmem_limit_bytes=32 * 1024 * 1024
        ),
    )(block_flags, hamilton)


def solution(mesh):
    in_specs = (P("row", "col"), P("row", "col"))
    out_specs = P("row", "col")
    return jax.shard_map(body, mesh=mesh, in_specs=in_specs, out_specs=out_specs, check_vma=False)
```

```python
import jax
import jax.numpy as jnp
from jax import lax
from jax.experimental import pallas as pl
from jax.experimental.pallas import tpu as pltpu
from jax.sharding import PartitionSpec as P

MESH = pl.DeviceIdType.MESH
NX, NY, NZL, NZH, NC = 4, 4, 8, 4, 2
NZ = NZL * NZH
BS = 64
WIDE = 256
HALF = 128
ORDER = 4096

P1, P2, P3, P4 = 0, 1, 2, 3
ROW_P, ROW_L, ROW_R, ROW_LF, ROW_RF, ROW_Y0, ROW_Y1, ROW_Y2 = 4, 5, 6, 7, 8, 9, 10, 11
COL = 12
ADD1 = 18
FIRST = 19
ADD2 = 25
N_SEM = 26


def kernel(flag_hbm, h_hbm, out_ref, flag_ref, h_ref, mine, panel, rowp, firstp, xrow, part, got,
           p1, p2, p3, p4, local, send, recv):
    row = lax.axis_index("row")
    col = lax.axis_index("col")
    x = lax.div(row, NZL * NC)
    zl = lax.rem(lax.div(row, NC), NZL)
    c = lax.rem(row, NC)
    y = lax.div(col, NZH)
    zh = lax.rem(col, NZH)
    z = zh * NZL + zl
    p = lax.rem(zl, 2)
    hz = lax.div(zl, 2)
    near = lax.div(hz, 2) * 2
    far = 2 - near
    side = 1 - 2 * p
    left = lax.rem(zh + 3, NZH)
    right = lax.rem(zh + 1, NZH)
    across = lax.rem(zh + 2, NZH)

    def dev(x=x, y=y, zl=zl, zh=zh, c=c):
        return ((x * NZL + zl) * NC + c, y * NZH + zh)

    def z_peer(d):
        at = lax.rem(z + d + NZ, NZ)
        return dev(zl=lax.rem(at, NZL), zh=lax.div(at, NZL))

    def x_peer(d):
        return dev(x=lax.rem(x + d, NX))

    def y_peer(d):
        return dev(y=lax.rem(y + d, NY))

    def xc_peer(d):
        at = lax.rem(x * NC + c + d, NX * NC)
        return dev(x=lax.div(at, NC), c=lax.rem(at, NC))

    def put(ref, k, to, dst=None):
        pltpu.make_async_remote_copy(
            src_ref=ref,
            dst_ref=ref if dst is None else dst,
            send_sem=send.at[k],
            recv_sem=recv.at[k],
            device_id=to,
            device_id_type=MESH,
        ).start()

    def take(view, k):
        pltpu.make_async_copy(view, view, recv.at[k]).wait()

    def sent(view, k):
        pltpu.make_async_copy(view, view, send.at[k]).wait()

    fetch = pltpu.make_async_copy(h_hbm, h_ref, local.at[0])
    fetch.start()
    fetch_flags = pltpu.make_async_copy(flag_hbm, flag_ref, local.at[1])
    fetch_flags.start()

    barrier = pltpu.get_barrier_semaphore()

    def greet(first, last, peer):
        def step(d, carry):
            pl.semaphore_signal(barrier, inc=1, device_id=peer(d), device_id_type=MESH)
            return carry

        lax.fori_loop(first, last, step, 0)

    pl.semaphore_signal(barrier, inc=1, device_id=z_peer(9 * side), device_id_type=MESH)
    greet(1, 9, z_peer)
    greet(-8, 0, z_peer)
    greet(1, NX * NC, xc_peer)
    greet(1, NY, y_peer)

    fetch.wait()
    fetch_flags.wait()
    for b in range(4):
        block = h_ref[:, b * BS:(b + 1) * BS]
        block = jnp.where(flag_ref[0, b] > 0, block, jnp.zeros_like(block))
        panel[x, hz, c, :, b * BS:(b + 1) * BS] = block
        mine[b // 2, :, (b % 2) * BS:(b % 2 + 1) * BS] = block
    rowp[y, zh, p] = mine[p]
    wide0 = mine[0].astype(jnp.float32)
    wide1 = mine[1].astype(jnp.float32)
    p1[x * NC + c] = jnp.sum(wide0 * wide0 + wide1 * wide1, axis=0, keepdims=True)

    pl.semaphore_wait(barrier, 17 + (NX * NC - 1) + (NY - 1))

    mate = zl + side
    for d in range(1, NX * NC):
        put(p1.at[x * NC + c], P1, xc_peer(d))
    slot = rowp.at[y, zh, p]
    for way, k in ((right, ROW_L), (left, ROW_R)):
        put(mine.at[1 - p], k, dev(zl=mate, zh=way), slot)
        put(mine.at[p], k, dev(zh=way), slot)
    put(mine.at[1 - p], ROW_P, dev(zl=mate), slot)

    def over_z(ref, k):
        own = ref.at[x, hz, c]
        for d in range(2):
            put(own, k + 1, dev(zl=2 * (far + lax.rem(hz + d, 2)) + p))
        put(own, k, dev(zl=2 * (near + lax.rem(hz + 1, 2)) + p))

    def over_x(ref, k, batch):
        take(ref.at[0, pl.ds(0, 1 + batch), 0], k + batch)
        lines = ref.at[x, pl.ds(far if batch else near, 2), c]
        for d in (2, 1, 3):
            put(lines, k + 2 + batch, x_peer(d))

    def over_core(ref, k, batch):
        take(ref.at[pl.ds(0, 3), pl.ds(0, 2), 0], k + 2 + batch)
        put(ref.at[:, pl.ds(far if batch else near, 2), c], k + 4 + batch, dev(c=1 - c))

    def have(ref, k, batch):
        take(ref.at[:, pl.ds(0, 2), 0], k + 4 + batch)

    def settled(ref, k):
        for batch in range(2):
            sent(ref.at[0, pl.ds(0, 1 + batch), 0], k + batch)
            sent(ref.at[pl.ds(0, 3), pl.ds(0, 2), 0], k + 2 + batch)
            sent(ref.at[:, pl.ds(0, 2), 0], k + 4 + batch)

    over_z(panel, COL)

    take(slot, ROW_P)
    for d in range(1, NY):
        put(rowp.at[y, zh], ROW_Y0, y_peer(d))
    take(p1.at[pl.ds(0, 7)], P1)
    p2[y] = jnp.sum(p1[...], axis=0)
    for d in range(1, NY):
        put(p2.at[y], P2, y_peer(d))
    over_x(panel, COL, 0)
    take(p2.at[pl.ds(0, 3)], P2)
    p3[7] = jnp.sum(p2[...], axis=0)
    for d in range(-8, 8):
        if d != 0:
            put(p3.at[7], P3, z_peer(d), p3.at[7 - d])

    over_x(panel, COL, 1)
    over_core(panel, COL, 0)
    take(rowp.at[y, left], ROW_L)
    put(rowp.at[y, left, 0], ROW_LF, dev(zh=right))
    take(rowp.at[y, right], ROW_R)
    put(rowp.at[y, right, 1], ROW_RF, dev(zh=left))
    for d in range(1, NY):
        put(rowp.at[y, left], ROW_Y1, y_peer(d))
        put(rowp.at[y, right], ROW_Y1, y_peer(d))
    over_core(panel, COL, 1)

    take(p3.at[pl.ds(0, 15)], P3)
    p4[2] = jnp.sum(p3[...], axis=0)
    put(p4.at[2], P4, dev(zh=right), p4.at[0])
    put(p4.at[2], P4, dev(zh=left), p4.at[1])

    take(slot, ROW_LF)
    take(slot, ROW_RF)
    for d in range(1, NY):
        put(rowp.at[y, across], ROW_Y2, y_peer(d))

    take(p4.at[pl.ds(0, 2)], P4)
    squares = jnp.sum(p4[0] + p4[1], axis=1, keepdims=True)
    factor = jnp.sqrt(jnp.float32(ORDER) / squares)
    have(panel, COL, 0)
    have(panel, COL, 1)
    take(rowp.at[0, pl.ds(0, 3)], ROW_Y0)
    take(rowp.at[pl.ds(0, 3), pl.ds(0, 2)], ROW_Y1)
    take(rowp.at[0, pl.ds(0, 3)], ROW_Y2)

    def scaled(value):
        return (value.astype(jnp.float32) * factor).astype(jnp.bfloat16)

    acc = jnp.zeros((2 * BS, WIDE), jnp.float32)
    for i in range(NY):
        for h in range(0, NZH, 2):
            lhs = jnp.concatenate([rowp[i, h].reshape(2 * BS, HALF), rowp[i, h + 1].reshape(2 * BS, HALF)], axis=1)
            lhs = scaled(lhs)
            xrow[i, h // 2] = lhs
            rhs = scaled(panel[i, h:h + 2].reshape(WIDE, WIDE))
            acc += jnp.dot(lhs, rhs, preferred_element_type=jnp.float32)
    part[...] = acc.reshape(2, BS, WIDE)
    put(part.at[1 - p], ADD1, dev(zl=mate), got.at[0])
    own = scaled(panel[x, hz, c]).astype(jnp.float32)
    take(got.at[0], ADD1)
    firstp[x, hz, c] = (part[p] + got[0]).astype(jnp.bfloat16)

    over_z(firstp, FIRST)
    over_x(firstp, FIRST, 0)
    over_x(firstp, FIRST, 1)
    over_core(firstp, FIRST, 0)
    over_core(firstp, FIRST, 1)
    have(firstp, FIRST, 0)
    sent(part.at[0], ADD1)
    have(firstp, FIRST, 1)

    acc = jnp.zeros((2 * BS, WIDE), jnp.float32)
    for i in range(NY):
        for h in range(0, NZH, 2):
            rhs = firstp[i, h:h + 2].reshape(WIDE, WIDE)
            acc += jnp.dot(xrow[i, h // 2], rhs, preferred_element_type=jnp.float32)
    part[...] = acc.reshape(2, BS, WIDE)
    put(part.at[1 - p], ADD2, dev(zl=mate), got.at[1])
    settled(panel, COL)
    settled(firstp, FIRST)
    sent(p1.at[pl.ds(0, 7)], P1)
    sent(p2.at[pl.ds(0, 3)], P2)
    sent(p3.at[pl.ds(0, 15)], P3)
    sent(p4.at[pl.ds(0, 2)], P4)
    sent(slot, ROW_P)
    sent(rowp.at[0, 0], ROW_L)
    sent(rowp.at[0, 0], ROW_R)
    sent(slot, ROW_LF)
    sent(slot, ROW_RF)
    sent(rowp.at[0, pl.ds(0, 3)], ROW_Y0)
    sent(rowp.at[pl.ds(0, 3), pl.ds(0, 2)], ROW_Y1)
    sent(rowp.at[0, pl.ds(0, 3)], ROW_Y2)
    take(got.at[1], ADD2)
    out_ref[...] = 16.0 * (1.5 * own - 0.5 * (part[p] + got[1]))
    sent(part.at[0], ADD2)


SCRATCH = [
    pltpu.SMEM((1, 4), jnp.int32),
    pltpu.VMEM((BS, WIDE), jnp.bfloat16),
    pltpu.VMEM((2, BS, HALF), jnp.bfloat16),
    pltpu.VMEM((NX, NZH, NC, BS, WIDE), jnp.bfloat16),
    pltpu.VMEM((NY, NZH, 2, BS, HALF), jnp.bfloat16),
    pltpu.VMEM((NX, NZH, NC, BS, WIDE), jnp.bfloat16),
    pltpu.VMEM((NY, 2, 2 * BS, WIDE), jnp.bfloat16),
    pltpu.VMEM((2, BS, WIDE), jnp.float32),
    pltpu.VMEM((2, BS, WIDE), jnp.float32),
    pltpu.VMEM((NX * NC, 1, 128), jnp.float32),
    pltpu.VMEM((NY, 1, 128), jnp.float32),
    pltpu.VMEM((16, 1, 128), jnp.float32),
    pltpu.VMEM((3, 1, 128), jnp.float32),
    pltpu.SemaphoreType.DMA((2,)),
    pltpu.SemaphoreType.DMA((N_SEM,)),
    pltpu.SemaphoreType.DMA((N_SEM,)),
]


def body(hamilton, block_flags):
    return pl.pallas_call(
        kernel,
        out_shape=jax.ShapeDtypeStruct((BS, WIDE), jnp.float32),
        in_specs=[pl.BlockSpec(memory_space=pl.ANY)] * 2,
        out_specs=pl.BlockSpec(memory_space=pltpu.VMEM),
        scratch_shapes=SCRATCH,
        compiler_params=pltpu.CompilerParams(collective_id=0, has_side_effects=True),
    )(block_flags, hamilton)


def solution(mesh):
    in_specs = (P("row", "col"), P("row", "col"))
    out_specs = P("row", "col")
    return jax.shard_map(body, mesh=mesh, in_specs=in_specs, out_specs=out_specs, check_vma=False)
```

```python
import jax
import jax.numpy as jnp
from jax import lax
from jax.experimental import pallas as pl
from jax.experimental.pallas import tpu as pltpu
from jax.sharding import PartitionSpec as P

MESH = pl.DeviceIdType.MESH
NX, NY, NZL, NZH, NC = 4, 4, 8, 4, 2
NZ = NZL * NZH
BS = 64
WIDE = 256
HALF = 128
ORDER = 4096

LEFT, OWN, RIGHT, ACROSS = 0, 1, 2, 3

P1, P2, P3, P4 = 0, 1, 2, 3
ROW_P, ROW_L, ROW_R, ROW_LF, ROW_RF, ROW_Y1, ROW_Y2 = 4, 5, 6, 7, 8, 9, 10
COL = 12
ADD1 = 18
FIRST = 19
ADD2 = 25
N_SEM = 26


def kernel(flag_hbm, h_hbm, out_ref, flag_ref, h_ref, mine, panel, rowp, firstp, xrow, part, got,
           p1, p2, p3, p4, local, send, recv):
    row = lax.axis_index("row")
    col = lax.axis_index("col")
    x = lax.div(row, NZL * NC)
    zl = lax.rem(lax.div(row, NC), NZL)
    c = lax.rem(row, NC)
    y = lax.div(col, NZH)
    zh = lax.rem(col, NZH)
    z = zh * NZL + zl
    p = lax.rem(zl, 2)
    hz = lax.div(zl, 2)
    near = lax.div(hz, 2) * 2
    far = 2 - near
    side = 1 - 2 * p
    left = lax.rem(zh + 3, NZH)
    right = lax.rem(zh + 1, NZH)

    def dev(x=x, y=y, zl=zl, zh=zh, c=c):
        return ((x * NZL + zl) * NC + c, y * NZH + zh)

    def z_peer(d):
        at = lax.rem(z + d + NZ, NZ)
        return dev(zl=lax.rem(at, NZL), zh=lax.div(at, NZL))

    def x_peer(d):
        return dev(x=lax.rem(x + d, NX))

    def y_peer(d):
        return dev(y=lax.rem(y + d, NY))

    def xc_peer(d):
        at = lax.rem(x * NC + c + d, NX * NC)
        return dev(x=lax.div(at, NC), c=lax.rem(at, NC))

    def put(ref, k, to, dst=None):
        pltpu.make_async_remote_copy(
            src_ref=ref,
            dst_ref=ref if dst is None else dst,
            send_sem=send.at[k],
            recv_sem=recv.at[k],
            device_id=to,
            device_id_type=MESH,
        ).start()

    def take(view, k):
        pltpu.make_async_copy(view, view, recv.at[k]).wait()

    def sent(view, k):
        pltpu.make_async_copy(view, view, send.at[k]).wait()

    fetch = pltpu.make_async_copy(h_hbm, h_ref, local.at[0])
    fetch.start()
    fetch_flags = pltpu.make_async_copy(flag_hbm, flag_ref, local.at[1])
    fetch_flags.start()

    barrier = pltpu.get_barrier_semaphore()

    def greet(first, last, peer):
        def step(d, carry):
            pl.semaphore_signal(barrier, inc=1, device_id=peer(d), device_id_type=MESH)
            return carry

        lax.fori_loop(first, last, step, 0)

    pl.semaphore_signal(barrier, inc=1, device_id=z_peer(9 * side), device_id_type=MESH)
    greet(1, 9, z_peer)
    greet(-8, 0, z_peer)
    greet(1, NX * NC, xc_peer)
    greet(1, NY, y_peer)

    fetch.wait()
    fetch_flags.wait()
    for b in range(4):
        block = h_ref[:, b * BS:(b + 1) * BS]
        block = jnp.where(flag_ref[0, b] > 0, block, jnp.zeros_like(block))
        panel[x, hz, c, :, b * BS:(b + 1) * BS] = block
        mine[b // 2, :, (b % 2) * BS:(b % 2 + 1) * BS] = block
    rowp[y, OWN, p] = mine[p]
    wide0 = mine[0].astype(jnp.float32)
    wide1 = mine[1].astype(jnp.float32)
    p1[x * NC + c] = jnp.sum(wide0 * wide0 + wide1 * wide1, axis=0, keepdims=True)

    pl.semaphore_wait(barrier, 17 + (NX * NC - 1) + (NY - 1))

    mate = zl + side
    for d in range(1, NX * NC):
        put(p1.at[x * NC + c], P1, xc_peer(d))
    for way, k, at in ((right, ROW_L, LEFT), (left, ROW_R, RIGHT)):
        put(mine.at[1 - p], k, dev(zl=mate, zh=way), rowp.at[y, at, p])
        put(mine.at[p], k, dev(zh=way), rowp.at[y, at, p])
    put(mine.at[1 - p], ROW_P, dev(zl=mate), rowp.at[y, OWN, p])

    def over_z(ref, k):
        own = ref.at[x, hz, c]
        for d in range(2):
            put(own, k + 1, dev(zl=2 * (far + lax.rem(hz + d, 2)) + p))
        put(own, k, dev(zl=2 * (near + lax.rem(hz + 1, 2)) + p))

    def over_x(ref, k, batch):
        take(ref.at[0, pl.ds(0, 1 + batch), 0], k + batch)
        lines = ref.at[x, pl.ds(far if batch else near, 2), c]
        for d in (2, 1, 3):
            put(lines, k + 2 + batch, x_peer(d))

    def over_core(ref, k, batch):
        take(ref.at[pl.ds(0, 3), pl.ds(0, 2), 0], k + 2 + batch)
        put(ref.at[:, pl.ds(far if batch else near, 2), c], k + 4 + batch, dev(c=1 - c))

    def have(ref, k, batch):
        take(ref.at[:, pl.ds(0, 2), 0], k + 4 + batch)

    def settled(ref, k):
        for batch in range(2):
            sent(ref.at[0, pl.ds(0, 1 + batch), 0], k + batch)
            sent(ref.at[pl.ds(0, 3), pl.ds(0, 2), 0], k + 2 + batch)
            sent(ref.at[:, pl.ds(0, 2), 0], k + 4 + batch)

    over_z(panel, COL)

    take(p1.at[pl.ds(0, 7)], P1)
    p2[y] = jnp.sum(p1[...], axis=0)
    for d in range(1, NY):
        put(p2.at[y], P2, y_peer(d))
    take(p2.at[pl.ds(0, 3)], P2)
    p3[7] = jnp.sum(p2[...], axis=0)
    for d in range(-8, 8):
        if d != 0:
            put(p3.at[7], P3, z_peer(d), p3.at[7 - d])

    over_x(panel, COL, 0)
    take(rowp.at[y, LEFT], ROW_L)
    put(rowp.at[y, LEFT, 0], ROW_LF, dev(zh=right), rowp.at[y, ACROSS, 0])
    take(rowp.at[y, RIGHT], ROW_R)
    put(rowp.at[y, RIGHT, 1], ROW_RF, dev(zh=left), rowp.at[y, ACROSS, 1])
    take(rowp.at[y, OWN, 0], ROW_P)
    for d in (2, 1, 3):
        put(rowp.at[y, pl.ds(0, 3)], ROW_Y1, y_peer(d))
    over_x(panel, COL, 1)
    over_core(panel, COL, 0)
    take(p3.at[pl.ds(0, 15)], P3)
    p4[2] = jnp.sum(p3[...], axis=0)
    put(p4.at[2], P4, dev(zh=right), p4.at[0])
    put(p4.at[2], P4, dev(zh=left), p4.at[1])

    over_core(panel, COL, 1)

    take(rowp.at[y, ACROSS, 0], ROW_LF)
    take(rowp.at[y, ACROSS, 1], ROW_RF)
    for d in (2, 1, 3):
        put(rowp.at[y, ACROSS], ROW_Y2, y_peer(d))

    take(p4.at[pl.ds(0, 2)], P4)
    squares = jnp.sum(p4[0] + p4[1], axis=1, keepdims=True)
    factor = jnp.sqrt(jnp.float32(ORDER) / squares)
    have(panel, COL, 0)
    have(panel, COL, 1)
    take(rowp.at[pl.ds(0, 3), pl.ds(0, 3)], ROW_Y1)
    take(rowp.at[0, pl.ds(0, 3)], ROW_Y2)

    def scaled(value):
        return (value.astype(jnp.float32) * factor).astype(jnp.bfloat16)

    def deep(ref, i, h):
        parts = [ref[i, lax.rem(zh + 3 + at, NZH)].reshape(2 * BS, WIDE) for at in (h, h + 1)]
        return jnp.concatenate(parts, axis=0)

    acc = jnp.zeros((2 * BS, WIDE), jnp.float32)
    for i in range(NY):
        for h in range(0, NZH, 2):
            lhs = jnp.concatenate([rowp[i, h].reshape(2 * BS, HALF), rowp[i, h + 1].reshape(2 * BS, HALF)], axis=1)
            lhs = scaled(lhs)
            xrow[i, h // 2] = lhs
            rhs = scaled(deep(panel, i, h))
            acc += jnp.dot(lhs, rhs, preferred_element_type=jnp.float32)
    part[...] = acc.reshape(2, BS, WIDE)
    put(part.at[1 - p], ADD1, dev(zl=mate), got.at[0])
    own = scaled(panel[x, hz, c]).astype(jnp.float32)
    take(got.at[0], ADD1)
    firstp[x, hz, c] = (part[p] + got[0]).astype(jnp.bfloat16)

    over_z(firstp, FIRST)
    over_x(firstp, FIRST, 0)
    over_x(firstp, FIRST, 1)
    over_core(firstp, FIRST, 0)
    over_core(firstp, FIRST, 1)
    have(firstp, FIRST, 0)
    sent(part.at[0], ADD1)
    have(firstp, FIRST, 1)

    acc = jnp.zeros((2 * BS, WIDE), jnp.float32)
    for i in range(NY):
        for h in range(0, NZH, 2):
            rhs = deep(firstp, i, h)
            acc += jnp.dot(xrow[i, h // 2], rhs, preferred_element_type=jnp.float32)
    part[...] = acc.reshape(2, BS, WIDE)
    put(part.at[1 - p], ADD2, dev(zl=mate), got.at[1])
    settled(panel, COL)
    settled(firstp, FIRST)
    sent(p1.at[pl.ds(0, 7)], P1)
    sent(p2.at[pl.ds(0, 3)], P2)
    sent(p3.at[pl.ds(0, 15)], P3)
    sent(p4.at[pl.ds(0, 2)], P4)
    sent(mine.at[0], ROW_P)
    sent(rowp.at[0, 0], ROW_L)
    sent(rowp.at[0, 0], ROW_R)
    sent(mine.at[0], ROW_LF)
    sent(mine.at[0], ROW_RF)
    sent(rowp.at[pl.ds(0, 3), pl.ds(0, 3)], ROW_Y1)
    sent(rowp.at[0, pl.ds(0, 3)], ROW_Y2)
    take(got.at[1], ADD2)
    out_ref[...] = 16.0 * (1.5 * own - 0.5 * (part[p] + got[1]))
    sent(part.at[0], ADD2)


SCRATCH = [
    pltpu.SMEM((1, 4), jnp.int32),
    pltpu.VMEM((BS, WIDE), jnp.bfloat16),
    pltpu.VMEM((2, BS, HALF), jnp.bfloat16),
    pltpu.VMEM((NX, NZH, NC, BS, WIDE), jnp.bfloat16),
    pltpu.VMEM((NY, NZH, 2, BS, HALF), jnp.bfloat16),
    pltpu.VMEM((NX, NZH, NC, BS, WIDE), jnp.bfloat16),
    pltpu.VMEM((NY, 2, 2 * BS, WIDE), jnp.bfloat16),
    pltpu.VMEM((2, BS, WIDE), jnp.float32),
    pltpu.VMEM((2, BS, WIDE), jnp.float32),
    pltpu.VMEM((NX * NC, 1, 128), jnp.float32),
    pltpu.VMEM((NY, 1, 128), jnp.float32),
    pltpu.VMEM((16, 1, 128), jnp.float32),
    pltpu.VMEM((3, 1, 128), jnp.float32),
    pltpu.SemaphoreType.DMA((2,)),
    pltpu.SemaphoreType.DMA((N_SEM,)),
    pltpu.SemaphoreType.DMA((N_SEM,)),
]


def body(hamilton, block_flags):
    return pl.pallas_call(
        kernel,
        out_shape=jax.ShapeDtypeStruct((BS, WIDE), jnp.float32),
        in_specs=[pl.BlockSpec(memory_space=pl.ANY)] * 2,
        out_specs=pl.BlockSpec(memory_space=pltpu.VMEM),
        scratch_shapes=SCRATCH,
        compiler_params=pltpu.CompilerParams(collective_id=0, has_side_effects=True),
    )(block_flags, hamilton)


def solution(mesh):
    in_specs = (P("row", "col"), P("row", "col"))
    out_specs = P("row", "col")
    return jax.shard_map(body, mesh=mesh, in_specs=in_specs, out_specs=out_specs, check_vma=False)
```

```python
import jax
import jax.numpy as jnp
from jax import lax
from jax.experimental import pallas as pl
from jax.experimental.pallas import tpu as pltpu
from jax.sharding import PartitionSpec as P

MESH = pl.DeviceIdType.MESH
NX, NY, NZL, NZH, NC = 4, 4, 8, 4, 2
NZ = NZL * NZH
BS = 64
WIDE = 256
HALF = 128
ORDER = 4096

LEFT, OWN, RIGHT, ACROSS = 0, 1, 2, 3

P1, P2, P3, P4 = 0, 1, 2, 3
ROW_P, ROW_L, ROW_R, ROW_LF, ROW_RF, ROW_Y1, ROW_Y2 = 4, 5, 6, 7, 8, 9, 10
COL = 12
ADD1 = 18
FIRST = 19
ADD2 = 25
N_SEM = 26


def kernel(flag_hbm, h_hbm, out_ref, flag_ref, h_ref, mine, panel, rowp, firstp, xrow, xpanel, part, got,
           p1, p2, p3, p4, local, send, recv):
    row = lax.axis_index("row")
    col = lax.axis_index("col")
    x = lax.div(row, NZL * NC)
    zl = lax.rem(lax.div(row, NC), NZL)
    c = lax.rem(row, NC)
    y = lax.div(col, NZH)
    zh = lax.rem(col, NZH)
    z = zh * NZL + zl
    p = lax.rem(zl, 2)
    hz = lax.div(zl, 2)
    near = lax.div(hz, 2) * 2
    far = 2 - near
    side = 1 - 2 * p
    left = lax.rem(zh + 3, NZH)
    right = lax.rem(zh + 1, NZH)

    def dev(x=x, y=y, zl=zl, zh=zh, c=c):
        return ((x * NZL + zl) * NC + c, y * NZH + zh)

    def z_peer(d):
        at = lax.rem(z + d + NZ, NZ)
        return dev(zl=lax.rem(at, NZL), zh=lax.div(at, NZL))

    def x_peer(d):
        return dev(x=lax.rem(x + d, NX))

    def y_peer(d):
        return dev(y=lax.rem(y + d, NY))

    def xc_peer(d):
        at = lax.rem(x * NC + c + d, NX * NC)
        return dev(x=lax.div(at, NC), c=lax.rem(at, NC))

    def put(ref, k, to, dst=None):
        pltpu.make_async_remote_copy(
            src_ref=ref,
            dst_ref=ref if dst is None else dst,
            send_sem=send.at[k],
            recv_sem=recv.at[k],
            device_id=to,
            device_id_type=MESH,
        ).start()

    def take(view, k):
        pltpu.make_async_copy(view, view, recv.at[k]).wait()

    def sent(view, k):
        pltpu.make_async_copy(view, view, send.at[k]).wait()

    fetch = pltpu.make_async_copy(h_hbm, h_ref, local.at[0])
    fetch.start()
    fetch_flags = pltpu.make_async_copy(flag_hbm, flag_ref, local.at[1])
    fetch_flags.start()

    barrier = pltpu.get_barrier_semaphore()

    def greet(first, last, peer):
        def step(d, carry):
            pl.semaphore_signal(barrier, inc=1, device_id=peer(d), device_id_type=MESH)
            return carry

        lax.fori_loop(first, last, step, 0)

    pl.semaphore_signal(barrier, inc=1, device_id=z_peer(9 * side), device_id_type=MESH)
    greet(1, 9, z_peer)
    greet(-8, 0, z_peer)
    greet(1, NX * NC, xc_peer)
    greet(1, NY, y_peer)

    fetch.wait()
    fetch_flags.wait()
    for b in range(4):
        block = h_ref[:, b * BS:(b + 1) * BS]
        block = jnp.where(flag_ref[0, b] > 0, block, jnp.zeros_like(block))
        panel[x, hz, c, :, b * BS:(b + 1) * BS] = block
        mine[b // 2, :, (b % 2) * BS:(b % 2 + 1) * BS] = block
    rowp[y, OWN, p] = mine[p]
    wide0 = mine[0].astype(jnp.float32)
    wide1 = mine[1].astype(jnp.float32)
    p1[x * NC + c] = jnp.sum(wide0 * wide0 + wide1 * wide1, axis=0, keepdims=True)

    pl.semaphore_wait(barrier, 17 + (NX * NC - 1) + (NY - 1))

    mate = zl + side
    for d in range(1, NX * NC):
        put(p1.at[x * NC + c], P1, xc_peer(d))
    for way, k, at in ((right, ROW_L, LEFT), (left, ROW_R, RIGHT)):
        put(mine.at[1 - p], k, dev(zl=mate, zh=way), rowp.at[y, at, p])
        put(mine.at[p], k, dev(zh=way), rowp.at[y, at, p])
    put(mine.at[1 - p], ROW_P, dev(zl=mate), rowp.at[y, OWN, p])

    def over_z(ref, k):
        own = ref.at[x, hz, c]
        put(own, k, dev(zl=2 * (near + lax.rem(hz + 1, 2)) + p))
        for d in range(2):
            put(own, k + 1, dev(zl=2 * (far + lax.rem(hz + d, 2)) + p))

    def over_x(ref, k, batch):
        take(ref.at[0, pl.ds(0, 1 + batch), 0], k + batch)
        lines = ref.at[x, pl.ds(far if batch else near, 2), c]
        for d in (2, 1, 3):
            put(lines, k + 2 + batch, x_peer(d))

    def over_core(ref, k, batch):
        take(ref.at[pl.ds(0, 3), pl.ds(0, 2), 0], k + 2 + batch)
        put(ref.at[:, pl.ds(far if batch else near, 2), c], k + 4 + batch, dev(c=1 - c))

    def have(ref, k, batch):
        take(ref.at[:, pl.ds(0, 2), 0], k + 4 + batch)

    def settled(ref, k):
        for batch in range(2):
            sent(ref.at[0, pl.ds(0, 1 + batch), 0], k + batch)
            sent(ref.at[pl.ds(0, 3), pl.ds(0, 2), 0], k + 2 + batch)
            sent(ref.at[:, pl.ds(0, 2), 0], k + 4 + batch)

    over_z(panel, COL)

    take(p1.at[pl.ds(0, 7)], P1)
    p2[y] = jnp.sum(p1[...], axis=0)
    for d in range(1, NY):
        put(p2.at[y], P2, y_peer(d))
    take(p2.at[pl.ds(0, 3)], P2)
    p3[7] = jnp.sum(p2[...], axis=0)
    for d in range(-8, 8):
        if d != 0:
            put(p3.at[7], P3, z_peer(d), p3.at[7 - d])

    over_x(panel, COL, 0)
    take(rowp.at[y, LEFT], ROW_L)
    put(rowp.at[y, LEFT, 0], ROW_LF, dev(zh=right), rowp.at[y, ACROSS, 0])
    take(rowp.at[y, RIGHT], ROW_R)
    put(rowp.at[y, RIGHT, 1], ROW_RF, dev(zh=left), rowp.at[y, ACROSS, 1])
    take(rowp.at[y, OWN, 0], ROW_P)
    for d in (2, 1, 3):
        put(rowp.at[y, pl.ds(0, 3)], ROW_Y1, y_peer(d))
    over_x(panel, COL, 1)
    over_core(panel, COL, 0)
    take(p3.at[pl.ds(0, 15)], P3)
    p4[2] = jnp.sum(p3[...], axis=0)
    put(p4.at[2], P4, dev(zh=right), p4.at[0])
    put(p4.at[2], P4, dev(zh=left), p4.at[1])

    over_core(panel, COL, 1)

    take(rowp.at[y, ACROSS, 0], ROW_LF)
    take(rowp.at[y, ACROSS, 1], ROW_RF)
    for d in (2, 1, 3):
        put(rowp.at[y, ACROSS], ROW_Y2, y_peer(d))

    take(p4.at[pl.ds(0, 2)], P4)
    squares = jnp.sum(p4[0] + p4[1], axis=1, keepdims=True)
    factor = jnp.sqrt(jnp.float32(ORDER) / squares)
    have(panel, COL, 0)
    have(panel, COL, 1)
    take(rowp.at[pl.ds(0, 3), pl.ds(0, 3)], ROW_Y1)
    take(rowp.at[0, pl.ds(0, 3)], ROW_Y2)

    def scaled(value):
        return (value.astype(jnp.float32) * factor).astype(jnp.bfloat16)

    def deep(ref, i, h):
        parts = [ref[i, lax.rem(zh + 3 + at, NZH)].reshape(2 * BS, WIDE) for at in (h, h + 1)]
        return jnp.concatenate(parts, axis=0)

    def product(rows, columns):
        acc = jnp.zeros((BS, WIDE), jnp.float32)
        for i in range(NY):
            for h in range(0, NZH, 2):
                acc += jnp.dot(rows(i, h), columns(i, h), preferred_element_type=jnp.float32)
        return acc

    def fresh(at):
        def rows(i, h):
            lhs = scaled(jnp.concatenate([rowp[i, h, at], rowp[i, h + 1, at]], axis=1))
            xrow[i, h // 2, at] = lhs
            return lhs

        return rows

    def fresh_columns(i, h):
        rhs = scaled(deep(panel, i, h))
        xpanel[i, h // 2] = rhs
        return rhs

    part[0] = product(fresh(1 - p), fresh_columns)
    put(part.at[0], ADD1, dev(zl=mate), got.at[0])
    mid = product(fresh(p), lambda i, h: xpanel[i, h // 2])
    own = scaled(panel[x, hz, c]).astype(jnp.float32)
    take(got.at[0], ADD1)
    firstp[x, hz, c] = (mid + got[0]).astype(jnp.bfloat16)

    over_z(firstp, FIRST)
    over_x(firstp, FIRST, 0)
    over_x(firstp, FIRST, 1)
    over_core(firstp, FIRST, 0)
    over_core(firstp, FIRST, 1)
    have(firstp, FIRST, 0)
    sent(part.at[0], ADD1)
    have(firstp, FIRST, 1)

    part[1] = product(lambda i, h: xrow[i, h // 2, 1 - p], lambda i, h: deep(firstp, i, h))
    put(part.at[1], ADD2, dev(zl=mate), got.at[1])
    last = product(lambda i, h: xrow[i, h // 2, p], lambda i, h: deep(firstp, i, h))
    last = 1.5 * own - 0.5 * last
    settled(panel, COL)
    settled(firstp, FIRST)
    sent(p1.at[pl.ds(0, 7)], P1)
    sent(p2.at[pl.ds(0, 3)], P2)
    sent(p3.at[pl.ds(0, 15)], P3)
    sent(p4.at[pl.ds(0, 2)], P4)
    sent(mine.at[0], ROW_P)
    sent(rowp.at[0, 0], ROW_L)
    sent(rowp.at[0, 0], ROW_R)
    sent(mine.at[0], ROW_LF)
    sent(mine.at[0], ROW_RF)
    sent(rowp.at[pl.ds(0, 3), pl.ds(0, 3)], ROW_Y1)
    sent(rowp.at[0, pl.ds(0, 3)], ROW_Y2)
    take(got.at[1], ADD2)
    out_ref[...] = 16.0 * (last - 0.5 * got[1])
    sent(part.at[0], ADD2)


SCRATCH = [
    pltpu.SMEM((1, 4), jnp.int32),
    pltpu.VMEM((BS, WIDE), jnp.bfloat16),
    pltpu.VMEM((2, BS, HALF), jnp.bfloat16),
    pltpu.VMEM((NX, NZH, NC, BS, WIDE), jnp.bfloat16),
    pltpu.VMEM((NY, NZH, 2, BS, HALF), jnp.bfloat16),
    pltpu.VMEM((NX, NZH, NC, BS, WIDE), jnp.bfloat16),
    pltpu.VMEM((NY, 2, 2, BS, WIDE), jnp.bfloat16),
    pltpu.VMEM((NY, 2, WIDE, WIDE), jnp.bfloat16),
    pltpu.VMEM((2, BS, WIDE), jnp.float32),
    pltpu.VMEM((2, BS, WIDE), jnp.float32),
    pltpu.VMEM((NX * NC, 1, 128), jnp.float32),
    pltpu.VMEM((NY, 1, 128), jnp.float32),
    pltpu.VMEM((16, 1, 128), jnp.float32),
    pltpu.VMEM((3, 1, 128), jnp.float32),
    pltpu.SemaphoreType.DMA((2,)),
    pltpu.SemaphoreType.DMA((N_SEM,)),
    pltpu.SemaphoreType.DMA((N_SEM,)),
]


def body(hamilton, block_flags):
    return pl.pallas_call(
        kernel,
        out_shape=jax.ShapeDtypeStruct((BS, WIDE), jnp.float32),
        in_specs=[pl.BlockSpec(memory_space=pl.ANY)] * 2,
        out_specs=pl.BlockSpec(memory_space=pltpu.VMEM),
        scratch_shapes=SCRATCH,
        compiler_params=pltpu.CompilerParams(collective_id=0, has_side_effects=True, vmem_limit_bytes=48 * 1024 * 1024),
    )(block_flags, hamilton)


def solution(mesh):
    in_specs = (P("row", "col"), P("row", "col"))
    out_specs = P("row", "col")
    return jax.shard_map(body, mesh=mesh, in_specs=in_specs, out_specs=out_specs, check_vma=False)
```

```python
import jax
import jax.numpy as jnp
from jax import lax
from jax.experimental import pallas as pl
from jax.experimental.pallas import tpu as pltpu
from jax.sharding import PartitionSpec as P

MESH = pl.DeviceIdType.MESH
NX, NY, NZL, NZH, NC = 4, 4, 8, 4, 2
NZ = NZL * NZH
BS = 64
WIDE = 256
HALF = 128
ORDER = 4096

LEFT, OWN, RIGHT, ACROSS = 0, 1, 2, 3

P1, P2, P3, P4 = 0, 1, 2, 3
ROW_P, ROW_L, ROW_R, ROW_LF, ROW_RF, ROW_Y1, ROW_Y2 = 4, 5, 6, 7, 8, 9, 10
COL = 12
ADD1 = 18
FIRST = 19
ADD2 = 25
N_SEM = 26


def kernel(flag_hbm, h_hbm, out_ref, flag_ref, h_ref, mine, panel, rowp, firstp, xrow, xpanel, part, got,
           p1, p2, p3, p4, local, send, recv):
    row = lax.axis_index("row")
    col = lax.axis_index("col")
    x = lax.div(row, NZL * NC)
    zl = lax.rem(lax.div(row, NC), NZL)
    c = lax.rem(row, NC)
    y = lax.div(col, NZH)
    zh = lax.rem(col, NZH)
    z = zh * NZL + zl
    p = lax.rem(zl, 2)
    hz = lax.div(zl, 2)
    near = lax.div(hz, 2) * 2
    far = 2 - near
    side = 1 - 2 * p
    left = lax.rem(zh + 3, NZH)
    right = lax.rem(zh + 1, NZH)

    def dev(x=x, y=y, zl=zl, zh=zh, c=c):
        return ((x * NZL + zl) * NC + c, y * NZH + zh)

    def z_peer(d):
        at = lax.rem(z + d + NZ, NZ)
        return dev(zl=lax.rem(at, NZL), zh=lax.div(at, NZL))

    def x_peer(d):
        return dev(x=lax.rem(x + d, NX))

    def y_peer(d):
        return dev(y=lax.rem(y + d, NY))

    def xc_peer(d):
        at = lax.rem(x * NC + c + d, NX * NC)
        return dev(x=lax.div(at, NC), c=lax.rem(at, NC))

    def put(ref, k, to, dst=None):
        pltpu.make_async_remote_copy(
            src_ref=ref,
            dst_ref=ref if dst is None else dst,
            send_sem=send.at[k],
            recv_sem=recv.at[k],
            device_id=to,
            device_id_type=MESH,
        ).start()

    def take(view, k):
        pltpu.make_async_copy(view, view, recv.at[k]).wait()

    def sent(view, k):
        pltpu.make_async_copy(view, view, send.at[k]).wait()

    fetch = pltpu.make_async_copy(h_hbm, h_ref, local.at[0])
    fetch.start()
    fetch_flags = pltpu.make_async_copy(flag_hbm, flag_ref, local.at[1])
    fetch_flags.start()

    barrier = pltpu.get_barrier_semaphore()

    def greet(first, last, peer):
        def step(d, carry):
            pl.semaphore_signal(barrier, inc=1, device_id=peer(d), device_id_type=MESH)
            return carry

        lax.fori_loop(first, last, step, 0)

    pl.semaphore_signal(barrier, inc=1, device_id=z_peer(9 * side), device_id_type=MESH)
    greet(1, 9, z_peer)
    greet(-8, 0, z_peer)
    greet(1, NX * NC, xc_peer)
    greet(1, NY, y_peer)

    fetch.wait()
    fetch_flags.wait()
    for b in range(4):
        block = h_ref[:, b * BS:(b + 1) * BS]
        block = jnp.where(flag_ref[0, b] > 0, block, jnp.zeros_like(block))
        panel[x, hz, c, :, b * BS:(b + 1) * BS] = block
        mine[b // 2, :, (b % 2) * BS:(b % 2 + 1) * BS] = block
    rowp[y, OWN, p] = mine[p]
    wide0 = mine[0].astype(jnp.float32)
    wide1 = mine[1].astype(jnp.float32)
    p1[x * NC + c] = jnp.sum(wide0 * wide0 + wide1 * wide1, axis=0, keepdims=True)

    pl.semaphore_wait(barrier, 17 + (NX * NC - 1) + (NY - 1))

    mate = zl + side
    for d in range(1, NX * NC):
        put(p1.at[x * NC + c], P1, xc_peer(d))
    for way, k, at in ((right, ROW_L, LEFT), (left, ROW_R, RIGHT)):
        put(mine.at[1 - p], k, dev(zl=mate, zh=way), rowp.at[y, at, p])
    for way, k, at in ((right, ROW_L, LEFT), (left, ROW_R, RIGHT)):
        put(mine.at[p], k, dev(zh=way), rowp.at[y, at, p])
    put(mine.at[1 - p], ROW_P, dev(zl=mate), rowp.at[y, OWN, p])

    def over_z(ref, k):
        own = ref.at[x, hz, c]
        put(own, k, dev(zl=2 * (near + lax.rem(hz + 1, 2)) + p))
        for d in range(2):
            put(own, k + 1, dev(zl=2 * (far + lax.rem(hz + d, 2)) + p))

    def over_x(ref, k, batch):
        take(ref.at[0, pl.ds(0, 1 + batch), 0], k + batch)
        lines = ref.at[x, pl.ds(far if batch else near, 2), c]
        for d in (2, 1, 3):
            put(lines, k + 2 + batch, x_peer(d))

    def over_core(ref, k, batch):
        take(ref.at[pl.ds(0, 3), pl.ds(0, 2), 0], k + 2 + batch)
        put(ref.at[:, pl.ds(far if batch else near, 2), c], k + 4 + batch, dev(c=1 - c))

    def have(ref, k, batch):
        take(ref.at[:, pl.ds(0, 2), 0], k + 4 + batch)

    def settled(ref, k):
        for batch in range(2):
            sent(ref.at[0, pl.ds(0, 1 + batch), 0], k + batch)
            sent(ref.at[pl.ds(0, 3), pl.ds(0, 2), 0], k + 2 + batch)
            sent(ref.at[:, pl.ds(0, 2), 0], k + 4 + batch)

    over_z(panel, COL)

    take(p1.at[pl.ds(0, 7)], P1)
    p2[y] = jnp.sum(p1[...], axis=0)
    for d in range(1, NY):
        put(p2.at[y], P2, y_peer(d))
    take(p2.at[pl.ds(0, 3)], P2)
    p3[7] = jnp.sum(p2[...], axis=0)
    for d in range(-8, 8):
        if d != 0:
            put(p3.at[7], P3, z_peer(d), p3.at[7 - d])

    over_x(panel, COL, 0)
    take(rowp.at[y, LEFT], ROW_L)
    put(rowp.at[y, LEFT, 0], ROW_LF, dev(zh=right), rowp.at[y, ACROSS, 0])
    take(rowp.at[y, RIGHT], ROW_R)
    put(rowp.at[y, RIGHT, 1], ROW_RF, dev(zh=left), rowp.at[y, ACROSS, 1])
    take(rowp.at[y, OWN, 0], ROW_P)
    for d in (2, 1, 3):
        put(rowp.at[y, pl.ds(0, 3)], ROW_Y1, y_peer(d))
    over_x(panel, COL, 1)
    over_core(panel, COL, 0)
    take(p3.at[pl.ds(0, 15)], P3)
    p4[2] = jnp.sum(p3[...], axis=0)
    put(p4.at[2], P4, dev(zh=right), p4.at[0])
    put(p4.at[2], P4, dev(zh=left), p4.at[1])

    over_core(panel, COL, 1)

    take(rowp.at[y, ACROSS, 0], ROW_LF)
    take(rowp.at[y, ACROSS, 1], ROW_RF)
    for d in (2, 1, 3):
        put(rowp.at[y, ACROSS], ROW_Y2, y_peer(d))

    take(p4.at[pl.ds(0, 2)], P4)
    squares = jnp.sum(p4[0] + p4[1], axis=1, keepdims=True)
    factor = jnp.sqrt(jnp.float32(ORDER) / squares)
    have(panel, COL, 0)
    have(panel, COL, 1)
    take(rowp.at[pl.ds(0, 3), pl.ds(0, 3)], ROW_Y1)
    take(rowp.at[0, pl.ds(0, 3)], ROW_Y2)

    def scaled(value):
        return (value.astype(jnp.float32) * factor).astype(jnp.bfloat16)

    starts = (near, far)

    def deep(ref, i, half):
        return ref[i, pl.ds(starts[half], 2)].reshape(WIDE, WIDE)

    def product(rows, columns, halves=(0, 1)):
        acc = jnp.zeros((BS, WIDE), jnp.float32)
        for half in halves:
            for i in range(NY):
                acc += jnp.dot(rows(i, half), columns(i, half), preferred_element_type=jnp.float32)
        return acc

    def fresh(at):
        def rows(i, half):
            place = lax.rem(starts[half] - zh + 1 + NZH, NZH)
            after = lax.rem(place + 1, NZH)
            lhs = scaled(jnp.concatenate([rowp[i, place, at], rowp[i, after, at]], axis=1))
            xrow[i, half, at] = lhs
            return lhs

        return rows

    def fresh_columns(i, half):
        rhs = scaled(deep(panel, i, half))
        xpanel[i, half] = rhs
        return rhs

    part[0] = product(fresh(1 - p), fresh_columns)
    put(part.at[0], ADD1, dev(zl=mate), got.at[0])
    mid = product(fresh(p), lambda i, half: xpanel[i, half])
    own = scaled(panel[x, hz, c]).astype(jnp.float32)
    take(got.at[0], ADD1)
    firstp[x, hz, c] = (mid + got[0]).astype(jnp.bfloat16)

    over_z(firstp, FIRST)
    over_x(firstp, FIRST, 0)
    over_x(firstp, FIRST, 1)
    over_core(firstp, FIRST, 0)
    over_core(firstp, FIRST, 1)
    def kept(at):
        return lambda i, half: xrow[i, half, at]

    def squared(i, half):
        return deep(firstp, i, half)

    have(firstp, FIRST, 0)
    part[1] = product(kept(1 - p), squared, (0,))
    last = product(kept(p), squared, (0,))
    sent(part.at[0], ADD1)
    have(firstp, FIRST, 1)
    part[1] += product(kept(1 - p), squared, (1,))
    put(part.at[1], ADD2, dev(zl=mate), got.at[1])
    last += product(kept(p), squared, (1,))
    last = 1.5 * own - 0.5 * last
    settled(panel, COL)
    settled(firstp, FIRST)
    sent(p1.at[pl.ds(0, 7)], P1)
    sent(p2.at[pl.ds(0, 3)], P2)
    sent(p3.at[pl.ds(0, 15)], P3)
    sent(p4.at[pl.ds(0, 2)], P4)
    sent(mine.at[0], ROW_P)
    sent(rowp.at[0, 0], ROW_L)
    sent(rowp.at[0, 0], ROW_R)
    sent(mine.at[0], ROW_LF)
    sent(mine.at[0], ROW_RF)
    sent(rowp.at[pl.ds(0, 3), pl.ds(0, 3)], ROW_Y1)
    sent(rowp.at[0, pl.ds(0, 3)], ROW_Y2)
    take(got.at[1], ADD2)
    out_ref[...] = 16.0 * (last - 0.5 * got[1])
    sent(part.at[0], ADD2)


SCRATCH = [
    pltpu.SMEM((1, 4), jnp.int32),
    pltpu.VMEM((BS, WIDE), jnp.bfloat16),
    pltpu.VMEM((2, BS, HALF), jnp.bfloat16),
    pltpu.VMEM((NX, NZH, NC, BS, WIDE), jnp.bfloat16),
    pltpu.VMEM((NY, NZH, 2, BS, HALF), jnp.bfloat16),
    pltpu.VMEM((NX, NZH, NC, BS, WIDE), jnp.bfloat16),
    pltpu.VMEM((NY, 2, 2, BS, WIDE), jnp.bfloat16),
    pltpu.VMEM((NY, 2, WIDE, WIDE), jnp.bfloat16),
    pltpu.VMEM((2, BS, WIDE), jnp.float32),
    pltpu.VMEM((2, BS, WIDE), jnp.float32),
    pltpu.VMEM((NX * NC, 1, 128), jnp.float32),
    pltpu.VMEM((NY, 1, 128), jnp.float32),
    pltpu.VMEM((16, 1, 128), jnp.float32),
    pltpu.VMEM((3, 1, 128), jnp.float32),
    pltpu.SemaphoreType.DMA((2,)),
    pltpu.SemaphoreType.DMA((N_SEM,)),
    pltpu.SemaphoreType.DMA((N_SEM,)),
]


def body(hamilton, block_flags):
    return pl.pallas_call(
        kernel,
        out_shape=jax.ShapeDtypeStruct((BS, WIDE), jnp.float32),
        in_specs=[pl.BlockSpec(memory_space=pl.ANY)] * 2,
        out_specs=pl.BlockSpec(memory_space=pltpu.VMEM),
        scratch_shapes=SCRATCH,
        compiler_params=pltpu.CompilerParams(collective_id=0, has_side_effects=True, vmem_limit_bytes=48 * 1024 * 1024),
    )(block_flags, hamilton)


def solution(mesh):
    in_specs = (P("row", "col"), P("row", "col"))
    out_specs = P("row", "col")
    return jax.shard_map(body, mesh=mesh, in_specs=in_specs, out_specs=out_specs, check_vma=False)
```

```python
import jax
import jax.numpy as jnp
from jax import lax
from jax.experimental import pallas as pl
from jax.experimental.pallas import tpu as pltpu
from jax.sharding import PartitionSpec as P

MESH = pl.DeviceIdType.MESH
NX, NY, NZL, NZH, NC = 4, 4, 8, 4, 2
NZ = NZL * NZH
BS = 64
WIDE = 256
HALF = 128
ORDER = 4096

LEFT, OWN, RIGHT, ACROSS = 0, 1, 2, 3

P1, P2, P3, P4 = 0, 1, 2, 3
ROW_P, ROW_L, ROW_R, ROW_LF, ROW_RF, ROW_Y1, ROW_Y2 = 4, 5, 6, 7, 8, 9, 10
COL = 12
ADD1 = 18
FIRST = 19
ADD2 = 25
N_SEM = 26


def kernel(flag_hbm, h_hbm, out_ref, flag_ref, h_ref, mine, panel, rowp, firstp, xrow, xpanel, part, got,
           p1, p2, p3, p4, local, send, recv):
    row = lax.axis_index("row")
    col = lax.axis_index("col")
    x = lax.div(row, NZL * NC)
    zl = lax.rem(lax.div(row, NC), NZL)
    c = lax.rem(row, NC)
    y = lax.div(col, NZH)
    zh = lax.rem(col, NZH)
    z = zh * NZL + zl
    p = lax.rem(zl, 2)
    hz = lax.div(zl, 2)
    near = lax.div(hz, 2) * 2
    far = 2 - near
    side = 1 - 2 * p
    left = lax.rem(zh + 3, NZH)
    right = lax.rem(zh + 1, NZH)

    def dev(x=x, y=y, zl=zl, zh=zh, c=c):
        return ((x * NZL + zl) * NC + c, y * NZH + zh)

    def z_peer(d):
        at = lax.rem(z + d + NZ, NZ)
        return dev(zl=lax.rem(at, NZL), zh=lax.div(at, NZL))

    def x_peer(d):
        return dev(x=lax.rem(x + d, NX))

    def y_peer(d):
        return dev(y=lax.rem(y + d, NY))

    def xc_peer(d):
        at = lax.rem(x * NC + c + d, NX * NC)
        return dev(x=lax.div(at, NC), c=lax.rem(at, NC))

    def put(ref, k, to, dst=None):
        pltpu.make_async_remote_copy(
            src_ref=ref,
            dst_ref=ref if dst is None else dst,
            send_sem=send.at[k],
            recv_sem=recv.at[k],
            device_id=to,
            device_id_type=MESH,
        ).start()

    def take(view, k):
        pltpu.make_async_copy(view, view, recv.at[k]).wait()

    def sent(view, k):
        pltpu.make_async_copy(view, view, send.at[k]).wait()

    fetch = pltpu.make_async_copy(h_hbm, h_ref, local.at[0])
    fetch.start()
    fetch_flags = pltpu.make_async_copy(flag_hbm, flag_ref, local.at[1])
    fetch_flags.start()

    barrier = pltpu.get_barrier_semaphore()

    def greet(first, last, peer):
        def step(d, carry):
            pl.semaphore_signal(barrier, inc=1, device_id=peer(d), device_id_type=MESH)
            return carry

        lax.fori_loop(first, last, step, 0)

    pl.semaphore_signal(barrier, inc=1, device_id=z_peer(9 * side), device_id_type=MESH)
    greet(1, 9, z_peer)
    greet(-8, 0, z_peer)
    greet(1, NX * NC, xc_peer)
    greet(1, NY, y_peer)

    fetch.wait()
    fetch_flags.wait()
    for b in range(4):
        block = h_ref[:, b * BS:(b + 1) * BS]
        block = jnp.where(flag_ref[0, b] > 0, block, jnp.zeros_like(block))
        panel[x, hz, c, :, b * BS:(b + 1) * BS] = block
        mine[b // 2, :, (b % 2) * BS:(b % 2 + 1) * BS] = block
    rowp[y, OWN, p] = mine[p]
    wide0 = mine[0].astype(jnp.float32)
    wide1 = mine[1].astype(jnp.float32)
    p1[x * NC + c] = jnp.sum(wide0 * wide0 + wide1 * wide1, axis=0, keepdims=True)

    pl.semaphore_wait(barrier, 17 + (NX * NC - 1) + (NY - 1))

    mate = zl + side
    for d in range(1, NX * NC):
        put(p1.at[x * NC + c], P1, xc_peer(d))
    for way, k, at in ((right, ROW_L, LEFT), (left, ROW_R, RIGHT)):
        put(mine.at[1 - p], k, dev(zl=mate, zh=way), rowp.at[y, at, p])
    for way, k, at in ((right, ROW_L, LEFT), (left, ROW_R, RIGHT)):
        put(mine.at[p], k, dev(zh=way), rowp.at[y, at, p])
    put(mine.at[1 - p], ROW_P, dev(zl=mate), rowp.at[y, OWN, p])

    def over_z(ref, k):
        own = ref.at[x, hz, c]
        put(own, k, dev(zl=2 * (near + lax.rem(hz + 1, 2)) + p))
        for d in range(2):
            put(own, k + 1, dev(zl=2 * (far + lax.rem(hz + d, 2)) + p))

    def over_x(ref, k, batch):
        take(ref.at[0, pl.ds(0, 1 + batch), 0], k + batch)
        lines = ref.at[x, pl.ds(far if batch else near, 2), c]
        for d in (2, 1, 3):
            put(lines, k + 2 + batch, x_peer(d))

    def over_core(ref, k, batch):
        take(ref.at[pl.ds(0, 3), pl.ds(0, 2), 0], k + 2 + batch)
        put(ref.at[:, pl.ds(far if batch else near, 2), c], k + 4 + batch, dev(c=1 - c))

    def have(ref, k, batch):
        take(ref.at[:, pl.ds(0, 2), 0], k + 4 + batch)

    def settled(ref, k):
        for batch in range(2):
            sent(ref.at[0, pl.ds(0, 1 + batch), 0], k + batch)
            sent(ref.at[pl.ds(0, 3), pl.ds(0, 2), 0], k + 2 + batch)
            sent(ref.at[:, pl.ds(0, 2), 0], k + 4 + batch)

    over_z(panel, COL)

    take(p1.at[pl.ds(0, 7)], P1)
    p2[y] = jnp.sum(p1[...], axis=0)
    for d in range(1, NY):
        put(p2.at[y], P2, y_peer(d))
    take(p2.at[pl.ds(0, 3)], P2)
    p3[7] = jnp.sum(p2[...], axis=0)
    for d in range(-8, 8):
        if d != 0:
            put(p3.at[7], P3, z_peer(d), p3.at[7 - d])

    over_x(panel, COL, 0)
    take(rowp.at[y, LEFT], ROW_L)
    put(rowp.at[y, LEFT, 0], ROW_LF, dev(zh=right), rowp.at[y, ACROSS, 0])
    take(rowp.at[y, RIGHT], ROW_R)
    put(rowp.at[y, RIGHT, 1], ROW_RF, dev(zh=left), rowp.at[y, ACROSS, 1])
    take(rowp.at[y, OWN, 0], ROW_P)
    for d in (2, 1, 3):
        put(rowp.at[y, pl.ds(0, 3)], ROW_Y1, y_peer(d))
    over_x(panel, COL, 1)
    take(p3.at[pl.ds(0, 15)], P3)
    p4[2] = jnp.sum(p3[...], axis=0)
    put(p4.at[2], P4, dev(zh=right), p4.at[0])
    put(p4.at[2], P4, dev(zh=left), p4.at[1])

    take(panel.at[pl.ds(0, 3), pl.ds(0, 2), 0], COL + 2)
    take(panel.at[pl.ds(0, 3), pl.ds(0, 2), 0], COL + 3)
    put(panel.at[:, :, c], COL + 4, dev(c=1 - c))

    take(rowp.at[y, ACROSS, 0], ROW_LF)
    take(rowp.at[y, ACROSS, 1], ROW_RF)
    for d in (2, 1, 3):
        put(rowp.at[y, ACROSS], ROW_Y2, y_peer(d))

    take(p4.at[pl.ds(0, 2)], P4)
    squares = jnp.sum(p4[0] + p4[1], axis=1, keepdims=True)
    factor = jnp.sqrt(jnp.float32(ORDER) / squares)
    take(panel.at[:, :, 0], COL + 4)
    take(rowp.at[pl.ds(0, 3), pl.ds(0, 3)], ROW_Y1)
    take(rowp.at[0, pl.ds(0, 3)], ROW_Y2)

    def scaled(value):
        return (value.astype(jnp.float32) * factor).astype(jnp.bfloat16)

    starts = (near, far)

    def deep(ref, i, half):
        return ref[i, pl.ds(starts[half], 2)].reshape(WIDE, WIDE)

    def product(rows, columns, halves=(0, 1)):
        acc = jnp.zeros((BS, WIDE), jnp.float32)
        for half in halves:
            for i in range(NY):
                acc += jnp.dot(rows(i, half), columns(i, half), preferred_element_type=jnp.float32)
        return acc

    def fresh(at):
        def rows(i, half):
            place = lax.rem(starts[half] - zh + 1 + NZH, NZH)
            after = lax.rem(place + 1, NZH)
            lhs = scaled(jnp.concatenate([rowp[i, place, at], rowp[i, after, at]], axis=1))
            xrow[i, half, at] = lhs
            return lhs

        return rows

    def fresh_columns(i, half):
        rhs = scaled(deep(panel, i, half))
        xpanel[i, half] = rhs
        return rhs

    part[0] = product(fresh(1 - p), fresh_columns)
    put(part.at[0], ADD1, dev(zl=mate), got.at[0])
    mid = product(fresh(p), lambda i, half: xpanel[i, half])
    own = scaled(panel[x, hz, c]).astype(jnp.float32)
    take(got.at[0], ADD1)
    firstp[x, hz, c] = (mid + got[0]).astype(jnp.bfloat16)

    over_z(firstp, FIRST)
    over_x(firstp, FIRST, 0)
    over_x(firstp, FIRST, 1)
    over_core(firstp, FIRST, 0)
    over_core(firstp, FIRST, 1)
    def kept(at):
        return lambda i, half: xrow[i, half, at]

    def squared(i, half):
        return deep(firstp, i, half)

    have(firstp, FIRST, 0)
    part[1] = product(kept(1 - p), squared, (0,))
    last = product(kept(p), squared, (0,))
    sent(part.at[0], ADD1)
    have(firstp, FIRST, 1)
    part[1] += product(kept(1 - p), squared, (1,))
    put(part.at[1], ADD2, dev(zl=mate), got.at[1])
    last += product(kept(p), squared, (1,))
    last = 1.5 * own - 0.5 * last
    sent(panel.at[0, 0, 0], COL)
    sent(panel.at[0, pl.ds(0, 2), 0], COL + 1)
    sent(panel.at[pl.ds(0, 3), pl.ds(0, 2), 0], COL + 2)
    sent(panel.at[pl.ds(0, 3), pl.ds(0, 2), 0], COL + 3)
    sent(panel.at[:, :, 0], COL + 4)
    settled(firstp, FIRST)
    sent(p1.at[pl.ds(0, 7)], P1)
    sent(p2.at[pl.ds(0, 3)], P2)
    sent(p3.at[pl.ds(0, 15)], P3)
    sent(p4.at[pl.ds(0, 2)], P4)
    sent(mine.at[0], ROW_P)
    sent(rowp.at[0, 0], ROW_L)
    sent(rowp.at[0, 0], ROW_R)
    sent(mine.at[0], ROW_LF)
    sent(mine.at[0], ROW_RF)
    sent(rowp.at[pl.ds(0, 3), pl.ds(0, 3)], ROW_Y1)
    sent(rowp.at[0, pl.ds(0, 3)], ROW_Y2)
    take(got.at[1], ADD2)
    out_ref[...] = 16.0 * (last - 0.5 * got[1])
    sent(part.at[0], ADD2)


SCRATCH = [
    pltpu.SMEM((1, 4), jnp.int32),
    pltpu.VMEM((BS, WIDE), jnp.bfloat16),
    pltpu.VMEM((2, BS, HALF), jnp.bfloat16),
    pltpu.VMEM((NX, NZH, NC, BS, WIDE), jnp.bfloat16),
    pltpu.VMEM((NY, NZH, 2, BS, HALF), jnp.bfloat16),
    pltpu.VMEM((NX, NZH, NC, BS, WIDE), jnp.bfloat16),
    pltpu.VMEM((NY, 2, 2, BS, WIDE), jnp.bfloat16),
    pltpu.VMEM((NY, 2, WIDE, WIDE), jnp.bfloat16),
    pltpu.VMEM((2, BS, WIDE), jnp.float32),
    pltpu.VMEM((2, BS, WIDE), jnp.float32),
    pltpu.VMEM((NX * NC, 1, 128), jnp.float32),
    pltpu.VMEM((NY, 1, 128), jnp.float32),
    pltpu.VMEM((16, 1, 128), jnp.float32),
    pltpu.VMEM((3, 1, 128), jnp.float32),
    pltpu.SemaphoreType.DMA((2,)),
    pltpu.SemaphoreType.DMA((N_SEM,)),
    pltpu.SemaphoreType.DMA((N_SEM,)),
]


def body(hamilton, block_flags):
    return pl.pallas_call(
        kernel,
        out_shape=jax.ShapeDtypeStruct((BS, WIDE), jnp.float32),
        in_specs=[pl.BlockSpec(memory_space=pl.ANY)] * 2,
        out_specs=pl.BlockSpec(memory_space=pltpu.VMEM),
        scratch_shapes=SCRATCH,
        compiler_params=pltpu.CompilerParams(collective_id=0, has_side_effects=True, vmem_limit_bytes=48 * 1024 * 1024),
    )(block_flags, hamilton)


def solution(mesh):
    in_specs = (P("row", "col"), P("row", "col"))
    out_specs = P("row", "col")
    return jax.shard_map(body, mesh=mesh, in_specs=in_specs, out_specs=out_specs, check_vma=False)
```
